256 devices in a mesh: walkers: 4 (over x_hi, core), band: 64 (over z, y, x_lo).
Axes of the slice: x: 4 (x_hi: 2, x_lo: 2; x = x_hi * 2 + x_lo), y: 4, z: 8, core: 2. Of those that a mesh axis runs over, the one named last changes fastest.
Arguments:
- orbitals: bfloat16 [256, 2048, 128], P(('walkers', 'band')), parts along dimension 0, may hold values from -6 to 6
Outputs:
- exchange: float32 [256, 2048, 128], P(('walkers', 'band')), parts along dimension 0
The draws below stay inside these ranges and needn't reach their ends.
There are 4 independent parts, one for each index of `walkers`. The reference program is written for one: setup_inputs(seed, part) draws one part's arguments, and reference() takes and returns one part's arrays. A program takes and returns all parts, laid end to end along the dimension named above; each array names one. Nothing has to cross between parts.
All inputs are finite; a program needn't handle non-finite values.
Results may differ from the reference program's by a relative error of at most 0.005.
The reference program's roundings to bfloat16 on the way count: a program that leaves them out, or rounds other values in their place, can miss the bound.
Values may be sent and summed in bfloat16 or wider, within the bound.
No kernel may reach another device: no remote copies, remote signals or barrier semaphores. Data moves between devices by JAX's collectives and lax.ppermute only.
A program may use at most 64 MiB of HBM per device.

```python
import math
import jax
import jax.numpy as jnp
from jax import lax

NG = 64
BAND_DEV = 1
HOPS = 3
BANDS = 64
N_BAND = 64


def block_levels(own_key, dims, cuts, least, high):
    def one(dim, blocks):
        heights = jax.random.uniform(jax.random.fold_in(jax.random.fold_in(own_key, 6), dim), (blocks,), jnp.float32, least / len(cuts), high / len(cuts))
        return jnp.repeat(jnp.exp(heights), dims[dim] // blocks).reshape((-1,) + (1,) * (len(dims) - dim - 1))

    factor_of = one(*cuts[0])
    for cut in cuts[1:]:
        factor_of = factor_of * one(*cut)
    return factor_of


def bell_draw(stream_key, extent, width, reach, split=(), held_as=jnp.bfloat16):
    gain = block_levels(stream_key, extent, split, -0.22, 0.18) if split else 1.0
    values = jax.random.normal(stream_key, extent, jnp.float32) * width * gain
    return jnp.minimum(jnp.maximum(values, -reach), reach).astype(held_as)


def setup_inputs(seed: int = 0, part: int = 0) -> dict:
    streams_of = jax.random.split(jax.random.key(seed), 2)
    part_splits = jax.random.split(jax.random.fold_in(streams_of[1], part), 2)
    orbitals = bell_draw(part_splits[0], (BANDS, NG * NG // 2, 2 * NG), 1.0, 6.0, ((0, 64),))
    return {"orbitals": orbitals}


MIXING = 0.25


def rounded(value):
    return lax.optimization_barrier(value.astype(jnp.bfloat16))


def product(form, left, right):
    return jnp.einsum(form, left.astype(jnp.float32), right.astype(jnp.float32))


def dft_tables(points):
    index_row = jnp.arange(points, dtype=jnp.int32)
    phase = (index_row[:, None] * index_row[None, :]) % points
    angle = phase.astype(jnp.float32) * (2.0 * math.pi / points)
    return jnp.cos(angle), jnp.sin(angle)


def coulomb_kernel(points):
    index_row = jnp.arange(points, dtype=jnp.int32)
    wave = jnp.where(index_row < points // 2, index_row, index_row - points)
    squared = wave[:, None, None] ** 2 + wave[None, :, None] ** 2 + wave[None, None, :] ** 2
    strength = points ** 1.5 / 4.0
    kernel = jnp.where(squared > 0, strength / jnp.maximum(squared, 1).astype(jnp.float32), 0.0)
    return kernel.astype(jnp.float32)


def potential(density):
    points = density.shape[1]
    cosine, sine = dft_tables(points)
    cos_table = rounded(cosine)
    sin_table = rounded(sine)
    along_z = "kz,pxyz->pxyk"
    along_y = "ky,pxyz->pxkz"
    along_x = "kx,pxyz->pkyz"
    first_real = rounded(product(along_z, cos_table, density))
    first_imag = rounded(-product(along_z, sin_table, density))
    second_real = rounded(product(along_y, cos_table, first_real) + product(along_y, sin_table, first_imag))
    second_imag = rounded(product(along_y, cos_table, first_imag) - product(along_y, sin_table, first_real))
    kernel = coulomb_kernel(points)[None]
    spec_real = product(along_x, cos_table, second_real) + product(along_x, sin_table, second_imag)
    spec_imag = product(along_x, cos_table, second_imag) - product(along_x, sin_table, second_real)
    spec_real = rounded(spec_real * kernel)
    spec_imag = rounded(spec_imag * kernel)
    one_real = rounded(product(along_x, cos_table, spec_real) - product(along_x, sin_table, spec_imag))
    one_imag = rounded(product(along_x, cos_table, spec_imag) + product(along_x, sin_table, spec_real))
    two_real = rounded(product(along_y, cos_table, one_real) - product(along_y, sin_table, one_imag))
    two_imag = rounded(product(along_y, cos_table, one_imag) + product(along_y, sin_table, one_real))
    field = product(along_z, cos_table, two_real) - product(along_z, sin_table, two_imag)
    return field * (1.0 / points ** 3)


def pair_terms(local_block, visiting):
    bands = local_block.shape[0]
    rows = local_block.shape[1]
    lanes = local_block.shape[2]
    points = lanes // 2
    density = rounded(local_block[:, None].astype(jnp.float32) * visiting[None].astype(jnp.float32))
    field = potential(density.reshape(bands * bands, points, points, points))
    field = field.reshape(bands, bands, rows, lanes)
    own_part = jnp.sum(field * visiting[None].astype(jnp.float32), axis=1)
    other_part = jnp.sum(field * local_block[:, None].astype(jnp.float32), axis=0)
    return own_part, other_part


def reference(orbitals):
    blocks = orbitals.reshape(N_BAND, BAND_DEV, NG * NG // 2, 2 * NG)
    total = jnp.zeros((N_BAND, BAND_DEV, NG * NG // 2, 2 * NG), jnp.float32)
    for offset in range(HOPS + 1):
        partner = jnp.roll(blocks, -offset, axis=0)

        def one_block(pair):
            return pair_terms(pair[0], pair[1])

        own_part, other_part = lax.map(one_block, (blocks, partner))
        total = total + own_part
        if offset > 0:
            total = total + jnp.roll(other_part, offset, axis=0)
    return (-MIXING * total).reshape(BANDS, NG * NG // 2, 2 * NG)
```

```python
import functools
import math

import jax
import jax.numpy as jnp
import ml_dtypes
import numpy as np
from jax import lax
from jax.experimental import pallas as pl
from jax.experimental.pallas import tpu as pltpu
from jax.sharding import PartitionSpec as P

NG = 64
HALF = 32
LANES = 128
SLOTS = 4
MIXING = 0.25


def dft_tables():
    index_row = np.arange(NG)
    angle = (index_row[:, None] * index_row[None, :] % NG).astype(np.float32)
    angle = angle * np.float32(2.0 * math.pi / NG)
    return [f(angle).astype(ml_dtypes.bfloat16).astype(np.float32) for f in (np.cos, np.sin)]


def paired(table_cos, table_sin, sign):
    return np.block([[table_cos, sign * table_sin], [-sign * table_sin, table_cos]])


def make_tables():
    cosine, sine = dft_tables()
    into = np.zeros((SLOTS, 2, NG, 2, 2, SLOTS, HALF), np.float32)
    back = np.zeros((2, 2, SLOTS, HALF, SLOTS, 2, NG), np.float32)
    for band in range(SLOTS):
        even = band - band % 2
        for parity in range(2):
            into[band, parity, :, parity, 0, band, 1:] = cosine[:, 1:HALF]
            into[band, parity, :, parity, 1, band, 1:] = -sine[:, 1:HALF]
            back[parity, 0, band, 1:, band, parity, :] = 2 * cosine[1:HALF]
            back[parity, 1, band, 1:, band, parity, :] = -2 * sine[1:HALF]
            for place, plane in ((even, 0), (even + 1, HALF)):
                into[band, parity, :, parity, band % 2, place, 0] = cosine[:, plane]
                back[parity, band % 2, place, 0, band, parity, :] = cosine[plane]
    into = into.reshape(SLOTS * LANES, SLOTS * LANES)
    back = back.reshape(SLOTS * LANES, SLOTS * LANES)
    order = np.arange(NG).reshape(HALF, 2).T
    y_in = np.concatenate([np.concatenate([order[b] + NG * c for c in range(2)]) for b in range(2)])
    forward = paired(cosine, sine, 1.0)
    inverse = paired(cosine, sine, -1.0)
    wave = np.arange(NG)
    wave = np.where(wave < HALF, wave, wave - NG)
    slots = np.tile(np.arange(HALF), (SLOTS, 1))
    slots[1::2, 0] = HALF
    squared = wave[:, None, None] ** 2 + wave[None, :, None] ** 2 + slots.reshape(-1)[None, None, :] ** 2
    strength = np.float32(NG**1.5 / 4.0)
    kernel = np.where(squared > 0, strength / np.maximum(squared, 1).astype(np.float32), np.float32(0))
    as_bf = lambda table: table.astype(ml_dtypes.bfloat16)
    return (
        as_bf(into),
        as_bf(forward[:, y_in]),
        as_bf(forward),
        kernel.reshape(NG * NG, LANES).astype(np.float32),
        as_bf(inverse),
        as_bf(inverse[y_in]),
        as_bf(back),
    )


def dot(left, right):
    return jnp.dot(left, right, preferred_element_type=jnp.float32)


def exchange_kernel(steps, own_ref, ahead_ref, behind_ref, *refs):
    into, y_fwd, x_fwd, kernel, x_inv, y_inv, back, out_ref, to_ahead, to_behind, planes, flat, spec = refs
    block, x_unroll = steps
    rows = block * HALF

    def wide(ref, base):
        return ref[pl.ds(base, rows), :].astype(jnp.float32)

    @pl.loop(0, NG // block)
    def _(at):
        base = pl.multiple_of(at * rows, rows)
        own, ahead, behind = (wide(ref, base) for ref in (own_ref, ahead_ref, behind_ref))
        density = [own * own, own * ahead, behind * own, behind * ahead]
        density = jnp.concatenate([d.astype(jnp.bfloat16) for d in density], axis=1)
        flat[...] = dot(density, into[...]).astype(jnp.bfloat16)
        for pair in range(block // 2):
            section = []
            for x in (2 * pair, 2 * pair + 1):
                section.append(
                    jnp.concatenate(
                        [flat[x * HALF : (x + 1) * HALF, t * LANES : (t + 1) * LANES] for t in range(4)], axis=0
                    )
                )
            second = dot(y_fwd[...], jnp.concatenate(section, axis=1))
            for n in range(2):
                place = pl.multiple_of((at * block + 2 * pair + n) * LANES, LANES)
                planes[pl.ds(place, LANES), :] = second[:, n * LANES : (n + 1) * LANES]

    @pl.loop(0, NG // (2 * x_unroll))
    def _(at):
        for pair in range(x_unroll):
            ky = (at * x_unroll + pair) * 2
            section = jnp.concatenate(
                [
                    jnp.concatenate(
                        [planes[pl.ds(ky + n + c * NG, NG, stride=LANES), :] for c in range(2)], axis=0
                    ).astype(jnp.bfloat16)
                    for n in range(2)
                ],
                axis=1,
            )
            spectrum = dot(x_fwd[...], section)
            weight = jnp.concatenate(
                [kernel[pl.ds(pl.multiple_of((ky + n) * NG, NG), NG), :] for n in range(2)], axis=1
            )
            weight = jnp.concatenate([weight, weight], axis=0)
            spectrum = (spectrum * weight).astype(jnp.bfloat16)
            back_one = dot(x_inv[...], spectrum)
            for n in range(2):
                place = pl.multiple_of((ky + n) * LANES, LANES)
                spec[pl.ds(place, LANES), :] = back_one[:, n * LANES : (n + 1) * LANES]

    @pl.loop(0, NG // block)
    def _(at):
        for pair in range(block // 2):
            x = at * block + 2 * pair
            section = jnp.concatenate(
                [
                    jnp.concatenate(
                        [spec[pl.ds(x + n + c * NG, NG, stride=LANES), :] for c in range(2)], axis=0
                    ).astype(jnp.bfloat16)
                    for n in range(2)
                ],
                axis=1,
            )
            back_two = dot(y_inv[...], section).astype(jnp.bfloat16)
            for n in range(2):
                row = (2 * pair + n) * HALF
                for t in range(4):
                    flat[row : row + HALF, t * LANES : (t + 1) * LANES] = back_two[
                        t * HALF : (t + 1) * HALF, n * LANES : (n + 1) * LANES
                    ]
        base = pl.multiple_of(at * rows, rows)
        field = dot(flat[...], back[...]) * (-MIXING / NG**3)
        alone, onward, rearward, across = (field[:, p * LANES : (p + 1) * LANES] for p in range(SLOTS))
        own, ahead, behind = (wide(ref, base) for ref in (own_ref, ahead_ref, behind_ref))
        out_ref[pl.ds(base, rows), :] = own * alone + ahead * onward + behind * rearward
        to_ahead[pl.ds(base, rows), :] = (own * onward + behind * across).astype(jnp.bfloat16)
        to_behind[pl.ds(base, rows), :] = (own * rearward + ahead * across).astype(jnp.bfloat16)


def exchange(own, ahead, behind, steps=(32, 16)):
    tables = [jnp.asarray(t) for t in make_tables()]
    operands = [own, ahead, behind, *tables]
    block = pl.BlockSpec(memory_space=pltpu.VMEM)
    return pl.pallas_call(
        functools.partial(exchange_kernel, steps),
        out_shape=[jax.ShapeDtypeStruct(own.shape, t) for t in (jnp.float32, jnp.bfloat16, jnp.bfloat16)],
        in_specs=[block] * len(operands),
        out_specs=[block] * 3,
        scratch_shapes=[
            pltpu.VMEM((NG * LANES, LANES), jnp.float32),
            pltpu.VMEM((steps[0] * HALF, SLOTS * LANES), jnp.bfloat16),
            pltpu.VMEM((NG * LANES, LANES), jnp.float32),
        ],
        compiler_params=pltpu.CompilerParams(vmem_limit_bytes=48 * 1024 * 1024),
        cost_estimate=pl.CostEstimate(flops=2**32, bytes_accessed=8 << 20, transcendentals=0),
    )(*operands)


def shifted(x, by):
    count = lax.axis_size("band")
    return lax.ppermute(x, "band", [(i, (i + by) % count) for i in range(count)])


def local(orbitals):
    own = orbitals[0]
    behind = shifted(own, 1)
    ahead = shifted(own, -2)
    total, to_ahead, to_behind = exchange(own, ahead, behind)
    total = total + shifted(to_behind, -1).astype(jnp.float32)
    total = total + shifted(to_ahead, 2).astype(jnp.float32)
    return total[None]


def solution(mesh):
    return jax.shard_map(
        local,
        mesh=mesh,
        in_specs=(P(("walkers", "band"), None, None),),
        out_specs=P(("walkers", "band"), None, None),
        check_vma=False,
    )
```

```python
import functools
import math

import jax
import jax.numpy as jnp
import ml_dtypes
import numpy as np
from jax import lax
from jax.experimental import pallas as pl
from jax.experimental.pallas import tpu as pltpu
from jax.sharding import PartitionSpec as P

NG = 64
HALF = 32
LANES = 128
SLOTS = 4
PITCH = 129
MIXING = 0.25


def dft_tables():
    index_row = np.arange(NG)
    angle = (index_row[:, None] * index_row[None, :] % NG).astype(np.float32)
    angle = angle * np.float32(2.0 * math.pi / NG)
    return [f(angle).astype(ml_dtypes.bfloat16).astype(np.float32) for f in (np.cos, np.sin)]


def paired(table_cos, table_sin, sign):
    return np.block([[table_cos, sign * table_sin], [-sign * table_sin, table_cos]])


def make_tables():
    cosine, sine = dft_tables()
    into = np.zeros((SLOTS, 2, NG, 2, 2, SLOTS, HALF), np.float32)
    back = np.zeros((2, 2, SLOTS, HALF, SLOTS, 2, NG), np.float32)
    for band in range(SLOTS):
        even = band - band % 2
        for parity in range(2):
            into[band, parity, :, parity, 0, band, 1:] = cosine[:, 1:HALF]
            into[band, parity, :, parity, 1, band, 1:] = -sine[:, 1:HALF]
            back[parity, 0, band, 1:, band, parity, :] = 2 * cosine[1:HALF]
            back[parity, 1, band, 1:, band, parity, :] = -2 * sine[1:HALF]
            for place, plane in ((even, 0), (even + 1, HALF)):
                into[band, parity, :, parity, band % 2, place, 0] = cosine[:, plane]
                back[parity, band % 2, place, 0, band, parity, :] = cosine[plane]
    into = into.reshape(SLOTS * LANES, SLOTS * LANES)
    back = back.reshape(SLOTS * LANES, SLOTS * LANES)
    order = np.arange(NG).reshape(HALF, 2).T
    y_in = np.concatenate([np.concatenate([order[b] + NG * c for c in range(2)]) for b in range(2)])
    forward = paired(cosine, sine, 1.0)
    inverse = paired(cosine, sine, -1.0)
    wave = np.arange(NG)
    wave = np.where(wave < HALF, wave, wave - NG)
    slots = np.tile(np.arange(HALF), (SLOTS, 1))
    slots[1::2, 0] = HALF
    squared = wave[:, None, None] ** 2 + wave[None, :, None] ** 2 + slots.reshape(-1)[None, None, :] ** 2
    strength = np.float32(NG**1.5 / 4.0)
    kernel = np.where(squared > 0, strength / np.maximum(squared, 1).astype(np.float32), np.float32(0))
    as_bf = lambda table: table.astype(ml_dtypes.bfloat16)
    return (
        as_bf(into),
        as_bf(forward[:, y_in]),
        as_bf(forward),
        kernel.reshape(NG * NG, LANES).astype(np.float32),
        as_bf(inverse),
        as_bf(inverse[y_in]),
        as_bf(back * np.float32(-MIXING / NG**3)),
    )


def dot(left, right):
    return jnp.dot(left, right, preferred_element_type=jnp.float32)


def exchange_kernel(steps, *refs):
    hbm_in, refs = refs[:10], refs[10:]
    hbm_out, refs = refs[:3], refs[3:]
    held_in, refs = refs[:10], refs[10:]
    held_out, refs = refs[:3], refs[3:]
    planes, spec, flat, in_sem, table_sem, out_sem = refs
    own_ref, ahead_ref, behind_ref, into, y_fwd, x_fwd, kernel, x_inv, y_inv, back = held_in
    out_ref, to_ahead, to_behind = held_out
    block, x_unroll = steps
    rows = block * HALF
    blocks = NG // block

    def part(at):
        return pl.ds(pl.multiple_of(at * rows, rows), rows)

    def arriving(which, at):
        return pltpu.make_async_copy(
            hbm_in[which].at[part(at)], held_in[which].at[part(at)], in_sem.at[which, at]
        )

    def table(which):
        return pltpu.make_async_copy(hbm_in[which], held_in[which], table_sem.at[which])

    def leaving(which, at):
        return pltpu.make_async_copy(
            held_out[which].at[part(at)], hbm_out[which].at[part(at)], out_sem.at[which, at]
        )

    table(3).start()
    for which in range(3):
        arriving(which, 0).start()
    table(4).start()
    for at in range(1, blocks):
        for which in range(3):
            arriving(which, at).start()
    for which in range(5, 10):
        table(which).start()
    table(3).wait()
    table(4).wait()

    def wide(ref, base):
        return ref[pl.ds(base, rows), :].astype(jnp.float32)

    @pl.loop(0, blocks)
    def _(at):
        for which in range(3):
            arriving(which, at).wait()
        base = pl.multiple_of(at * rows, rows)
        own, ahead, behind = (wide(ref, base) for ref in (own_ref, ahead_ref, behind_ref))
        density = [own * own, own * ahead, behind * own, behind * ahead]
        density = jnp.concatenate([d.astype(jnp.bfloat16) for d in density], axis=1)
        flat[...] = dot(density, into[...]).astype(jnp.bfloat16)
        for pair in range(block // 2):
            section = []
            for x in (2 * pair, 2 * pair + 1):
                section.append(
                    jnp.concatenate(
                        [flat[x * HALF : (x + 1) * HALF, t * LANES : (t + 1) * LANES] for t in range(4)], axis=0
                    )
                )
            second = dot(y_fwd[...], jnp.concatenate(section, axis=1))
            for n in range(2):
                place = (at * block + 2 * pair + n) * PITCH
                planes[pl.ds(place, LANES), :] = second[:, n * LANES : (n + 1) * LANES]

    for which in range(5, 10):
        table(which).wait()

    @pl.loop(0, NG // (2 * x_unroll))
    def _(at):
        for pair in range(x_unroll):
            ky = (at * x_unroll + pair) * 2
            section = jnp.concatenate(
                [
                    jnp.concatenate(
                        [planes[pl.ds(ky + n + c * NG, NG, stride=PITCH), :] for c in range(2)], axis=0
                    ).astype(jnp.bfloat16)
                    for n in range(2)
                ],
                axis=1,
            )
            spectrum = dot(x_fwd[...], section)
            weight = jnp.concatenate(
                [kernel[pl.ds(pl.multiple_of((ky + n) * NG, NG), NG), :] for n in range(2)], axis=1
            )
            weight = jnp.concatenate([weight, weight], axis=0)
            spectrum = (spectrum * weight).astype(jnp.bfloat16)
            back_one = dot(x_inv[...], spectrum)
            for n in range(2):
                spec[pl.ds((ky + n) * PITCH, LANES), :] = back_one[:, n * LANES : (n + 1) * LANES]

    @pl.loop(0, blocks)
    def _(at):
        for pair in range(block // 2):
            x = at * block + 2 * pair
            section = jnp.concatenate(
                [
                    jnp.concatenate(
                        [spec[pl.ds(x + n + c * NG, NG, stride=PITCH), :] for c in range(2)], axis=0
                    ).astype(jnp.bfloat16)
                    for n in range(2)
                ],
                axis=1,
            )
            back_two = dot(y_inv[...], section).astype(jnp.bfloat16)
            for n in range(2):
                row = (2 * pair + n) * HALF
                for t in range(4):
                    flat[row : row + HALF, t * LANES : (t + 1) * LANES] = back_two[
                        t * HALF : (t + 1) * HALF, n * LANES : (n + 1) * LANES
                    ]
        base = pl.multiple_of(at * rows, rows)
        field = dot(flat[...], back[...])
        alone, onward, rearward, across = (field[:, p * LANES : (p + 1) * LANES] for p in range(SLOTS))
        own, ahead, behind = (wide(ref, base) for ref in (own_ref, ahead_ref, behind_ref))
        to_ahead[pl.ds(base, rows), :] = (own * onward + behind * across).astype(jnp.bfloat16)
        to_behind[pl.ds(base, rows), :] = (own * rearward + ahead * across).astype(jnp.bfloat16)
        out_ref[pl.ds(base, rows), :] = own * alone + ahead * onward + behind * rearward
        for which in range(3):
            leaving(which, at).start()

    for at in range(blocks):
        for which in range(3):
            leaving(which, at).wait()


def exchange(own, ahead, behind, steps=(32, 32)):
    tables = [jnp.asarray(t) for t in make_tables()]
    operands = [own, ahead, behind, *tables]
    outputs = [jax.ShapeDtypeStruct(own.shape, t) for t in (jnp.float32, jnp.bfloat16, jnp.bfloat16)]
    blocks = NG // steps[0]
    return pl.pallas_call(
        functools.partial(exchange_kernel, steps),
        out_shape=outputs,
        in_specs=[pl.BlockSpec(memory_space=pl.ANY)] * len(operands),
        out_specs=[pl.BlockSpec(memory_space=pl.ANY)] * 3,
        scratch_shapes=[pltpu.VMEM(x.shape, x.dtype) for x in operands + outputs]
        + [
            pltpu.VMEM((NG * PITCH, LANES), jnp.float32),
            pltpu.VMEM((NG * PITCH, LANES), jnp.float32),
            pltpu.VMEM((steps[0] * HALF, SLOTS * LANES), jnp.bfloat16),
            pltpu.SemaphoreType.DMA((3, blocks)),
            pltpu.SemaphoreType.DMA((10,)),
            pltpu.SemaphoreType.DMA((3, blocks)),
        ],
        compiler_params=pltpu.CompilerParams(vmem_limit_bytes=60 * 1024 * 1024),
        cost_estimate=pl.CostEstimate(flops=2**32, bytes_accessed=8 << 20, transcendentals=0),
    )(*operands)


def shifted(x, by):
    count = lax.axis_size("band")
    return lax.ppermute(x, "band", [(i, (i + by) % count) for i in range(count)])


def local(orbitals):
    own = orbitals[0]
    behind = shifted(own, 1)
    ahead = shifted(own, -2)
    total, to_ahead, to_behind = exchange(own, ahead, behind)
    total = total + shifted(to_behind, -1).astype(jnp.float32)
    total = total + shifted(to_ahead, 2).astype(jnp.float32)
    return total[None]


def solution(mesh):
    return jax.shard_map(
        local,
        mesh=mesh,
        in_specs=(P(("walkers", "band"), None, None),),
        out_specs=P(("walkers", "band"), None, None),
        check_vma=False,
    )
```

```python
import functools
import math

import jax
import jax.numpy as jnp
import ml_dtypes
import numpy as np
from jax import lax
from jax.experimental import pallas as pl
from jax.experimental.pallas import tpu as pltpu
from jax.sharding import PartitionSpec as P

NG = 64
HALF = 32
LANES = 128
SLOTS = 4
PITCH = 129
MIXING = 0.25


def dft_tables():
    index_row = np.arange(NG)
    angle = (index_row[:, None] * index_row[None, :] % NG).astype(np.float32)
    angle = angle * np.float32(2.0 * math.pi / NG)
    return [f(angle).astype(ml_dtypes.bfloat16).astype(np.float32) for f in (np.cos, np.sin)]


def paired(table_cos, table_sin, sign):
    return np.block([[table_cos, sign * table_sin], [-sign * table_sin, table_cos]])


def make_tables():
    cosine, sine = dft_tables()
    into = np.zeros((SLOTS, 2, NG, 2, 2, SLOTS, HALF), np.float32)
    back = np.zeros((2, 2, SLOTS, HALF, SLOTS, 2, NG), np.float32)
    for band in range(SLOTS):
        even = band - band % 2
        for parity in range(2):
            into[band, parity, :, parity, 0, band, 1:] = cosine[:, 1:HALF]
            into[band, parity, :, parity, 1, band, 1:] = -sine[:, 1:HALF]
            back[parity, 0, band, 1:, band, parity, :] = 2 * cosine[1:HALF]
            back[parity, 1, band, 1:, band, parity, :] = -2 * sine[1:HALF]
            for place, plane in ((even, 0), (even + 1, HALF)):
                into[band, parity, :, parity, band % 2, place, 0] = cosine[:, plane]
                back[parity, band % 2, place, 0, band, parity, :] = cosine[plane]
    into = into.reshape(SLOTS * LANES, SLOTS * LANES)
    back = back.reshape(SLOTS * LANES, SLOTS * LANES)
    order = np.arange(NG).reshape(HALF, 2).T
    y_in = np.concatenate([np.concatenate([order[b] + NG * c for c in range(2)]) for b in range(2)])
    forward = paired(cosine, sine, 1.0)
    inverse = paired(cosine, sine, -1.0)
    wave = np.arange(NG)
    wave = np.where(wave < HALF, wave, wave - NG)
    slots = np.tile(np.arange(HALF), (SLOTS, 1))
    slots[1::2, 0] = HALF
    squared = wave[:, None, None] ** 2 + wave[None, :, None] ** 2 + slots.reshape(-1)[None, None, :] ** 2
    strength = np.float32(NG**1.5 / 4.0)
    kernel = np.where(squared > 0, strength / np.maximum(squared, 1).astype(np.float32), np.float32(0))
    as_bf = lambda table: table.astype(ml_dtypes.bfloat16)
    return (
        as_bf(into),
        as_bf(forward[:, y_in]),
        as_bf(forward),
        kernel.reshape(NG * NG, LANES).astype(np.float32),
        as_bf(inverse),
        as_bf(inverse[y_in]),
        as_bf(back * np.float32(-MIXING / NG**3)),
    )


def dot(left, right):
    return jnp.dot(left, right, preferred_element_type=jnp.float32)


def exchange_kernel(steps, own_ref, ahead_ref, behind_ref, *refs):
    into, y_fwd, x_fwd, kernel, x_inv, y_inv, back, out_ref, to_ahead, to_behind, planes, spec, flat = refs
    block, x_unroll = steps
    rows = block * HALF
    blocks = NG // block

    def wide(ref, base):
        return ref[pl.ds(base, rows), :].astype(jnp.float32)

    @pl.loop(0, blocks)
    def _(at):
        base = pl.multiple_of(at * rows, rows)
        own, ahead, behind = (wide(ref, base) for ref in (own_ref, ahead_ref, behind_ref))
        density = [own * own, own * ahead, behind * own, behind * ahead]
        density = jnp.concatenate([d.astype(jnp.bfloat16) for d in density], axis=1)
        flat[...] = dot(density, into[...]).astype(jnp.bfloat16)
        for pair in range(block // 2):
            section = []
            for x in (2 * pair, 2 * pair + 1):
                section.append(
                    jnp.concatenate(
                        [flat[x * HALF : (x + 1) * HALF, t * LANES : (t + 1) * LANES] for t in range(4)], axis=0
                    )
                )
            second = dot(y_fwd[...], jnp.concatenate(section, axis=1))
            for n in range(2):
                place = (at * block + 2 * pair + n) * PITCH
                planes[pl.ds(place, LANES), :] = second[:, n * LANES : (n + 1) * LANES]

    @pl.loop(0, NG // (2 * x_unroll))
    def _(at):
        for pair in range(x_unroll):
            ky = (at * x_unroll + pair) * 2
            section = jnp.concatenate(
                [
                    jnp.concatenate(
                        [planes[pl.ds(ky + n + c * NG, NG, stride=PITCH), :] for c in range(2)], axis=0
                    ).astype(jnp.bfloat16)
                    for n in range(2)
                ],
                axis=1,
            )
            spectrum = dot(x_fwd[...], section)
            weight = jnp.concatenate(
                [kernel[pl.ds(pl.multiple_of((ky + n) * NG, NG), NG), :] for n in range(2)], axis=1
            )
            weight = jnp.concatenate([weight, weight], axis=0)
            spectrum = (spectrum * weight).astype(jnp.bfloat16)
            back_one = dot(x_inv[...], spectrum)
            for n in range(2):
                spec[pl.ds((ky + n) * PITCH, LANES), :] = back_one[:, n * LANES : (n + 1) * LANES]

    @pl.loop(0, blocks)
    def _(at):
        for pair in range(block // 2):
            x = at * block + 2 * pair
            section = jnp.concatenate(
                [
                    jnp.concatenate(
                        [spec[pl.ds(x + n + c * NG, NG, stride=PITCH), :] for c in range(2)], axis=0
                    ).astype(jnp.bfloat16)
                    for n in range(2)
                ],
                axis=1,
            )
            back_two = dot(y_inv[...], section).astype(jnp.bfloat16)
            for n in range(2):
                row = (2 * pair + n) * HALF
                for t in range(4):
                    flat[row : row + HALF, t * LANES : (t + 1) * LANES] = back_two[
                        t * HALF : (t + 1) * HALF, n * LANES : (n + 1) * LANES
                    ]
        base = pl.multiple_of(at * rows, rows)
        field = dot(flat[...], back[...])
        alone, onward, rearward, across = (field[:, p * LANES : (p + 1) * LANES] for p in range(SLOTS))
        own, ahead, behind = (wide(ref, base) for ref in (own_ref, ahead_ref, behind_ref))
        to_ahead[pl.ds(base, rows), :] = (own * onward + behind * across).astype(jnp.bfloat16)
        to_behind[pl.ds(base, rows), :] = (own * rearward + ahead * across).astype(jnp.bfloat16)
        out_ref[pl.ds(base, rows), :] = own * alone + ahead * onward + behind * rearward


def hold_kernel(*refs):
    count = len(refs) // 2
    sources, held, sem = refs[:count], refs[count : 2 * count], refs[2 * count]
    copies = [pltpu.make_async_copy(s, h, sem.at[n]) for n, (s, h) in enumerate(zip(sources, held))]
    for copy in copies:
        copy.start()
    for copy in copies:
        copy.wait()


def held_in_vmem(arrays):
    return pl.pallas_call(
        hold_kernel,
        out_shape=[pltpu.VMEM(x.shape, x.dtype) for x in arrays],
        in_specs=[pl.BlockSpec(memory_space=pl.ANY)] * len(arrays),
        out_specs=[pl.BlockSpec(memory_space=pltpu.VMEM)] * len(arrays),
        scratch_shapes=[pltpu.SemaphoreType.DMA((len(arrays),))],
        compiler_params=pltpu.CompilerParams(vmem_limit_bytes=1024 * 1024),
        cost_estimate=pl.CostEstimate(flops=0, bytes_accessed=8 << 20, transcendentals=0),
    )(*arrays)


def exchange(own, ahead, behind, steps=(32, 32)):
    tables = [jnp.asarray(t) for t in make_tables()]
    own, *tables = held_in_vmem([own, *tables])
    operands = [own, ahead, behind, *tables]
    return pl.pallas_call(
        functools.partial(exchange_kernel, steps),
        out_shape=[jax.ShapeDtypeStruct(own.shape, t) for t in (jnp.float32, jnp.bfloat16, jnp.bfloat16)],
        in_specs=[pl.BlockSpec(memory_space=pltpu.VMEM)] * len(operands),
        out_specs=[pl.BlockSpec(memory_space=pltpu.VMEM)] * 3,
        scratch_shapes=[
            pltpu.VMEM((NG * PITCH, LANES), jnp.float32),
            pltpu.VMEM((NG * PITCH, LANES), jnp.float32),
            pltpu.VMEM((steps[0] * HALF, SLOTS * LANES), jnp.bfloat16),
        ],
        compiler_params=pltpu.CompilerParams(vmem_limit_bytes=24 * 1024 * 1024),
        cost_estimate=pl.CostEstimate(flops=2**32, bytes_accessed=8 << 20, transcendentals=0),
    )(*operands)


def shifted(x, by):
    count = lax.axis_size("band")
    return lax.ppermute(x, "band", [(i, (i + by) % count) for i in range(count)])


def local(orbitals):
    own = orbitals[0]
    behind = shifted(own, 1)
    ahead = shifted(own, -2)
    total, to_ahead, to_behind = exchange(own, ahead, behind)
    total = total + shifted(to_behind, -1).astype(jnp.float32)
    total = total + shifted(to_ahead, 2).astype(jnp.float32)
    return total[None]


def solution(mesh):
    return jax.shard_map(
        local,
        mesh=mesh,
        in_specs=(P(("walkers", "band"), None, None),),
        out_specs=P(("walkers", "band"), None, None),
        check_vma=False,
    )
```

```python
import functools
import math

import jax
import jax.numpy as jnp
import ml_dtypes
import numpy as np
from jax import lax
from jax.experimental import pallas as pl
from jax.experimental.pallas import tpu as pltpu
from jax.sharding import PartitionSpec as P

NG = 64
HALF = 32
LANES = 128
SLOTS = 4
PITCH = 129
MIXING = 0.25


def dft_tables():
    index_row = np.arange(NG)
    angle = (index_row[:, None] * index_row[None, :] % NG).astype(np.float32)
    angle = angle * np.float32(2.0 * math.pi / NG)
    return [f(angle).astype(ml_dtypes.bfloat16).astype(np.float32) for f in (np.cos, np.sin)]


def paired(table_cos, table_sin, sign):
    return np.block([[table_cos, sign * table_sin], [-sign * table_sin, table_cos]])


def make_tables():
    cosine, sine = dft_tables()
    into = np.zeros((SLOTS, 2, NG, 2, 2, SLOTS, HALF), np.float32)
    back = np.zeros((2, 2, SLOTS, HALF, SLOTS, 2, NG), np.float32)
    for band in range(SLOTS):
        even = band - band % 2
        for parity in range(2):
            into[band, parity, :, parity, 0, band, 1:] = cosine[:, 1:HALF]
            into[band, parity, :, parity, 1, band, 1:] = -sine[:, 1:HALF]
            back[parity, 0, band, 1:, band, parity, :] = 2 * cosine[1:HALF]
            back[parity, 1, band, 1:, band, parity, :] = -2 * sine[1:HALF]
            for place, plane in ((even, 0), (even + 1, HALF)):
                into[band, parity, :, parity, band % 2, place, 0] = cosine[:, plane]
                back[parity, band % 2, place, 0, band, parity, :] = cosine[plane]
    into = into.reshape(SLOTS * LANES, SLOTS * LANES)
    back = back.reshape(SLOTS * LANES, SLOTS * LANES)
    order = np.arange(NG).reshape(HALF, 2).T
    y_in = np.concatenate([np.concatenate([order[b] + NG * c for c in range(2)]) for b in range(2)])
    forward = paired(cosine, sine, 1.0)
    inverse = paired(cosine, sine, -1.0)
    wave = np.arange(NG)
    wave = np.where(wave < HALF, wave, wave - NG)
    slots = np.tile(np.arange(HALF), (SLOTS, 1))
    slots[1::2, 0] = HALF
    squared = wave[:, None, None] ** 2 + wave[None, :, None] ** 2 + slots.reshape(-1)[None, None, :] ** 2
    strength = np.float32(NG**1.5 / 4.0)
    kernel = np.where(squared > 0, strength / np.maximum(squared, 1).astype(np.float32), np.float32(0))
    as_bf = lambda table: table.astype(ml_dtypes.bfloat16)
    return (
        as_bf(into),
        as_bf(forward[:, y_in]),
        as_bf(forward),
        kernel.reshape(NG * NG, LANES).astype(np.float32),
        as_bf(inverse),
        as_bf(inverse[y_in]),
        as_bf(back * np.float32(-MIXING / NG**3)),
    )


def dot(left, right):
    return jnp.dot(left, right, preferred_element_type=jnp.float32)


def exchange_kernel(steps, own_ref, ahead_ref, behind_ref, *refs):
    into, y_fwd, x_fwd, kernel, x_inv, y_inv, back, out_ref, to_ahead, to_behind, planes, spec, flat = refs
    block, x_unroll = steps
    rows = block * HALF
    blocks = NG // block

    def wide(ref, base):
        return ref[pl.ds(base, rows), :].astype(jnp.float32)

    @pl.loop(0, blocks)
    def _(at):
        base = pl.multiple_of(at * rows, rows)
        own, ahead, behind = (wide(ref, base) for ref in (own_ref, ahead_ref, behind_ref))
        density = [own * own, own * ahead, behind * own, behind * ahead]
        density = jnp.concatenate([d.astype(jnp.bfloat16) for d in density], axis=1)
        flat[...] = dot(density, into[...]).astype(jnp.bfloat16)
        for pair in range(block // 2):
            section = []
            for x in (2 * pair, 2 * pair + 1):
                section.append(
                    jnp.concatenate(
                        [flat[x * HALF : (x + 1) * HALF, t * LANES : (t + 1) * LANES] for t in range(4)], axis=0
                    )
                )
            second = dot(y_fwd[...], jnp.concatenate(section, axis=1))
            for n in range(2):
                place = (at * block + 2 * pair + n) * PITCH
                planes[pl.ds(place, LANES), :] = second[:, n * LANES : (n + 1) * LANES]

    @pl.loop(0, NG // (2 * x_unroll))
    def _(at):
        for pair in range(x_unroll):
            ky = (at * x_unroll + pair) * 2
            section = jnp.concatenate(
                [
                    jnp.concatenate(
                        [planes[pl.ds(ky + n + c * NG, NG, stride=PITCH), :] for c in range(2)], axis=0
                    ).astype(jnp.bfloat16)
                    for n in range(2)
                ],
                axis=1,
            )
            spectrum = dot(x_fwd[...], section)
            weight = jnp.concatenate(
                [kernel[pl.ds(pl.multiple_of((ky + n) * NG, NG), NG), :] for n in range(2)], axis=1
            )
            weight = jnp.concatenate([weight, weight], axis=0)
            spectrum = (spectrum * weight).astype(jnp.bfloat16)
            back_one = dot(x_inv[...], spectrum)
            for n in range(2):
                spec[pl.ds((ky + n) * PITCH, LANES), :] = back_one[:, n * LANES : (n + 1) * LANES]

    @pl.loop(0, blocks)
    def _(at):
        for pair in range(block // 2):
            x = at * block + 2 * pair
            section = jnp.concatenate(
                [
                    jnp.concatenate(
                        [spec[pl.ds(x + n + c * NG, NG, stride=PITCH), :] for c in range(2)], axis=0
                    ).astype(jnp.bfloat16)
                    for n in range(2)
                ],
                axis=1,
            )
            back_two = dot(y_inv[...], section).astype(jnp.bfloat16)
            for n in range(2):
                row = (2 * pair + n) * HALF
                for t in range(4):
                    flat[row : row + HALF, t * LANES : (t + 1) * LANES] = back_two[
                        t * HALF : (t + 1) * HALF, n * LANES : (n + 1) * LANES
                    ]
        base = pl.multiple_of(at * rows, rows)
        field = dot(flat[...], back[...])
        alone, onward, rearward, across = (field[:, p * LANES : (p + 1) * LANES] for p in range(SLOTS))
        own, ahead, behind = (wide(ref, base) for ref in (own_ref, ahead_ref, behind_ref))
        to_ahead[pl.ds(base, rows), :] = (own * onward + behind * across).astype(jnp.bfloat16)
        to_behind[pl.ds(base, rows), :] = (own * rearward + ahead * across).astype(jnp.bfloat16)
        out_ref[pl.ds(base, rows), :] = own * alone + ahead * onward + behind * rearward


def hold_kernel(*refs):
    count = len(refs) // 2
    sources, held, sem = refs[:count], refs[count : 2 * count], refs[2 * count]
    copies = [pltpu.make_async_copy(s, h, sem.at[n]) for n, (s, h) in enumerate(zip(sources, held))]
    for copy in copies:
        copy.start()
    for copy in copies:
        copy.wait()


def held_in_vmem(arrays):
    return pl.pallas_call(
        hold_kernel,
        out_shape=[pltpu.VMEM(x.shape, x.dtype) for x in arrays],
        in_specs=[pl.BlockSpec(memory_space=pl.ANY)] * len(arrays),
        out_specs=[pl.BlockSpec(memory_space=pltpu.VMEM)] * len(arrays),
        scratch_shapes=[pltpu.SemaphoreType.DMA((len(arrays),))],
        compiler_params=pltpu.CompilerParams(vmem_limit_bytes=1024 * 1024),
        cost_estimate=pl.CostEstimate(flops=0, bytes_accessed=8 << 20, transcendentals=0),
    )(*arrays)


def exchange(own, ahead, behind, steps=(32, 32)):
    tables = [jnp.asarray(t) for t in make_tables()]
    own, *tables = held_in_vmem([own, *tables])
    operands = [own, ahead, behind, *tables]
    return pl.pallas_call(
        functools.partial(exchange_kernel, steps),
        out_shape=[jax.ShapeDtypeStruct(own.shape, t) for t in (jnp.float32, jnp.bfloat16, jnp.bfloat16)],
        in_specs=[pl.BlockSpec(memory_space=pltpu.VMEM)] * len(operands),
        out_specs=[pl.BlockSpec(memory_space=pltpu.VMEM)] * 3,
        scratch_shapes=[
            pltpu.VMEM((NG * PITCH, LANES), jnp.float32),
            pltpu.VMEM((NG * PITCH, LANES), jnp.float32),
            pltpu.VMEM((steps[0] * HALF, SLOTS * LANES), jnp.bfloat16),
        ],
        compiler_params=pltpu.CompilerParams(vmem_limit_bytes=24 * 1024 * 1024),
        cost_estimate=pl.CostEstimate(flops=2**32, bytes_accessed=8 << 20, transcendentals=0),
    )(*operands)


def shifted(x, by):
    count = lax.axis_size("band")
    return lax.ppermute(x, "band", [(i, (i + by) % count) for i in range(count)])


def local(orbitals):
    own = orbitals[0]
    behind = shifted(own, 1)
    ahead = shifted(own, -2)
    total, to_ahead, to_behind = exchange(own, ahead, behind)
    total = total + shifted(to_ahead, 2).astype(jnp.float32)
    total = total + shifted(to_behind, -1).astype(jnp.float32)
    return total[None]


def solution(mesh):
    return jax.shard_map(
        local,
        mesh=mesh,
        in_specs=(P(("walkers", "band"), None, None),),
        out_specs=P(("walkers", "band"), None, None),
        check_vma=False,
    )
```

```python
import functools
import math

import jax
import jax.numpy as jnp
import ml_dtypes
import numpy as np
from jax import lax
from jax.experimental import pallas as pl
from jax.experimental.pallas import tpu as pltpu
from jax.sharding import PartitionSpec as P

NG = 64
HALF = 32
LANES = 128
SLOTS = 4
PITCH = 129
MIXING = 0.25


def dft_tables():
    index_row = np.arange(NG)
    angle = (index_row[:, None] * index_row[None, :] % NG).astype(np.float32)
    angle = angle * np.float32(2.0 * math.pi / NG)
    return [f(angle).astype(ml_dtypes.bfloat16).astype(np.float32) for f in (np.cos, np.sin)]


def paired(table_cos, table_sin, sign):
    return np.block([[table_cos, sign * table_sin], [-sign * table_sin, table_cos]])


def make_tables():
    cosine, sine = dft_tables()
    into = np.zeros((SLOTS, 2, NG, 2, 2, SLOTS, HALF), np.float32)
    back = np.zeros((2, 2, SLOTS, HALF, SLOTS, 2, NG), np.float32)
    for band in range(SLOTS):
        even = band - band % 2
        for parity in range(2):
            into[band, parity, :, parity, 0, band, 1:] = cosine[:, 1:HALF]
            into[band, parity, :, parity, 1, band, 1:] = -sine[:, 1:HALF]
            back[parity, 0, band, 1:, band, parity, :] = 2 * cosine[1:HALF]
            back[parity, 1, band, 1:, band, parity, :] = -2 * sine[1:HALF]
            for place, plane in ((even, 0), (even + 1, HALF)):
                into[band, parity, :, parity, band % 2, place, 0] = cosine[:, plane]
                back[parity, band % 2, place, 0, band, parity, :] = cosine[plane]
    wide = 2 * LANES
    into_low = into[:2, :, :, :, :, :2].reshape(wide, wide)
    into_high = into[2:, :, :, :, ::-1, 2:].reshape(wide, wide)
    back_low = back[:, :, :2, :, :2].reshape(wide, wide)
    back_high = back[:, ::-1, 2:, :, 2:].reshape(wide, wide)
    order = np.arange(NG).reshape(HALF, 2).T
    y_in = np.concatenate([np.concatenate([order[b] + NG * c for c in range(2)]) for b in range(2)])
    forward = paired(cosine, sine, 1.0)
    inverse = paired(cosine, sine, -1.0)
    wave = np.arange(NG)
    wave = np.where(wave < HALF, wave, wave - NG)
    slots = np.tile(np.arange(HALF), (SLOTS, 1))
    slots[1::2, 0] = HALF
    squared = wave[:, None, None] ** 2 + wave[None, :, None] ** 2 + slots.reshape(-1)[None, None, :] ** 2
    strength = np.float32(NG**1.5 / 4.0)
    kernel = np.where(squared > 0, strength / np.maximum(squared, 1).astype(np.float32), np.float32(0))
    as_bf = lambda table: table.astype(ml_dtypes.bfloat16)
    return (
        as_bf(into_low),
        as_bf(into_high),
        as_bf(forward[:, y_in]),
        as_bf(forward),
        kernel.reshape(NG * NG, LANES).astype(np.float32),
        as_bf(inverse),
        as_bf(inverse[y_in]),
        as_bf(back_low * np.float32(-MIXING / NG**3)),
        as_bf(back_high * np.float32(-MIXING / NG**3)),
    )


def dot(left, right):
    return jnp.dot(left, right, preferred_element_type=jnp.float32)


def exchange_kernel(steps, own_ref, ahead_ref, behind_ref, *refs):
    into_low, into_high, y_fwd, x_fwd, kernel, x_inv, y_inv, back_low, back_high, *refs = refs
    out_ref, to_ahead, to_behind, planes, spec, flat = refs
    low = lax.broadcasted_iota(jnp.int32, (steps[0] * HALF, LANES), 1) < NG
    block, x_unroll = steps
    rows = block * HALF
    blocks = NG // block

    def wide(ref, base):
        return ref[pl.ds(base, rows), :].astype(jnp.float32)

    @pl.loop(0, blocks)
    def _(at):
        base = pl.multiple_of(at * rows, rows)
        own, ahead, behind = (wide(ref, base) for ref in (own_ref, ahead_ref, behind_ref))
        density = [own * own, own * ahead, behind * own, behind * ahead]
        density = [d.astype(jnp.bfloat16) for d in density]
        first = dot(jnp.concatenate(density[:2], axis=1), into_low[...])
        other = dot(jnp.concatenate(density[2:], axis=1), into_high[...])
        for parity in range(2):
            lanes = slice(parity * LANES, (parity + 1) * LANES)
            one, two = (x[:, lanes].astype(jnp.bfloat16) for x in (first, other))
            real = jnp.where(low, one, two)
            imag = jnp.where(low, two, one)
            imag = jnp.concatenate([imag[:, NG:], imag[:, :NG]], axis=1)
            flat[:, 2 * parity * LANES : (2 * parity + 1) * LANES] = real
            flat[:, (2 * parity + 1) * LANES : (2 * parity + 2) * LANES] = imag
        for pair in range(block // 2):
            section = []
            for x in (2 * pair, 2 * pair + 1):
                section.append(
                    jnp.concatenate(
                        [flat[x * HALF : (x + 1) * HALF, t * LANES : (t + 1) * LANES] for t in range(4)], axis=0
                    )
                )
            second = dot(y_fwd[...], jnp.concatenate(section, axis=1))
            for n in range(2):
                place = (at * block + 2 * pair + n) * PITCH
                planes[pl.ds(place, LANES), :] = second[:, n * LANES : (n + 1) * LANES]

    @pl.loop(0, NG // (2 * x_unroll))
    def _(at):
        for pair in range(x_unroll):
            ky = (at * x_unroll + pair) * 2
            section = jnp.concatenate(
                [
                    jnp.concatenate(
                        [planes[pl.ds(ky + n + c * NG, NG, stride=PITCH), :] for c in range(2)], axis=0
                    ).astype(jnp.bfloat16)
                    for n in range(2)
                ],
                axis=1,
            )
            spectrum = dot(x_fwd[...], section)
            weight = jnp.concatenate(
                [kernel[pl.ds(pl.multiple_of((ky + n) * NG, NG), NG), :] for n in range(2)], axis=1
            )
            weight = jnp.concatenate([weight, weight], axis=0)
            spectrum = (spectrum * weight).astype(jnp.bfloat16)
            back_one = dot(x_inv[...], spectrum)
            for n in range(2):
                spec[pl.ds((ky + n) * PITCH, LANES), :] = back_one[:, n * LANES : (n + 1) * LANES]

    @pl.loop(0, blocks)
    def _(at):
        for pair in range(block // 2):
            x = at * block + 2 * pair
            section = jnp.concatenate(
                [
                    jnp.concatenate(
                        [spec[pl.ds(x + n + c * NG, NG, stride=PITCH), :] for c in range(2)], axis=0
                    ).astype(jnp.bfloat16)
                    for n in range(2)
                ],
                axis=1,
            )
            back_two = dot(y_inv[...], section).astype(jnp.bfloat16)
            for n in range(2):
                row = (2 * pair + n) * HALF
                for parity in range(2):
                    lanes = slice(n * LANES, (n + 1) * LANES)
                    real = back_two[2 * parity * HALF : (2 * parity + 1) * HALF, lanes]
                    imag = back_two[(2 * parity + 1) * HALF : (2 * parity + 2) * HALF, lanes]
                    imag = jnp.concatenate([imag[:, NG:], imag[:, :NG]], axis=1)
                    for half, pick in enumerate((jnp.where(low[:HALF], real, imag), jnp.where(low[:HALF], imag, real))):
                        place = (2 * half + parity) * LANES
                        flat[row : row + HALF, place : place + LANES] = pick
        base = pl.multiple_of(at * rows, rows)
        alone, onward = jnp.split(dot(flat[:, : 2 * LANES], back_low[...]), 2, axis=1)
        rearward, across = jnp.split(dot(flat[:, 2 * LANES :], back_high[...]), 2, axis=1)
        own, ahead, behind = (wide(ref, base) for ref in (own_ref, ahead_ref, behind_ref))
        to_ahead[pl.ds(base, rows), :] = (own * onward + behind * across).astype(jnp.bfloat16)
        to_behind[pl.ds(base, rows), :] = (own * rearward + ahead * across).astype(jnp.bfloat16)
        out_ref[pl.ds(base, rows), :] = own * alone + ahead * onward + behind * rearward


def hold_kernel(*refs):
    count = len(refs) // 2
    sources, held, sem = refs[:count], refs[count : 2 * count], refs[2 * count]
    copies = [pltpu.make_async_copy(s, h, sem.at[n]) for n, (s, h) in enumerate(zip(sources, held))]
    for copy in copies:
        copy.start()
    for copy in copies:
        copy.wait()


def held_in_vmem(arrays):
    return pl.pallas_call(
        hold_kernel,
        out_shape=[pltpu.VMEM(x.shape, x.dtype) for x in arrays],
        in_specs=[pl.BlockSpec(memory_space=pl.ANY)] * len(arrays),
        out_specs=[pl.BlockSpec(memory_space=pltpu.VMEM)] * len(arrays),
        scratch_shapes=[pltpu.SemaphoreType.DMA((len(arrays),))],
        compiler_params=pltpu.CompilerParams(vmem_limit_bytes=1024 * 1024),
        cost_estimate=pl.CostEstimate(flops=0, bytes_accessed=8 << 20, transcendentals=0),
    )(*arrays)


def exchange(own, ahead, behind, steps=(64, 32)):
    tables = [jnp.asarray(t) for t in make_tables()]
    own, *tables = held_in_vmem([own, *tables])
    operands = [own, ahead, behind, *tables]
    return pl.pallas_call(
        functools.partial(exchange_kernel, steps),
        out_shape=[jax.ShapeDtypeStruct(own.shape, t) for t in (jnp.float32, jnp.bfloat16, jnp.bfloat16)],
        in_specs=[pl.BlockSpec(memory_space=pltpu.VMEM)] * len(operands),
        out_specs=[pl.BlockSpec(memory_space=pltpu.VMEM)] * 3,
        scratch_shapes=[
            pltpu.VMEM((NG * PITCH, LANES), jnp.float32),
            pltpu.VMEM((NG * PITCH, LANES), jnp.float32),
            pltpu.VMEM((steps[0] * HALF, SLOTS * LANES), jnp.bfloat16),
        ],
        compiler_params=pltpu.CompilerParams(vmem_limit_bytes=24 * 1024 * 1024),
        cost_estimate=pl.CostEstimate(flops=2**32, bytes_accessed=8 << 20, transcendentals=0),
    )(*operands)


def shifted(x, by):
    count = lax.axis_size("band")
    return lax.ppermute(x, "band", [(i, (i + by) % count) for i in range(count)])


def local(orbitals):
    own = orbitals[0]
    behind = shifted(own, 1)
    ahead = shifted(own, -2)
    total, to_ahead, to_behind = exchange(own, ahead, behind)
    total = total + shifted(to_ahead, 2).astype(jnp.float32)
    total = total + shifted(to_behind, -1).astype(jnp.float32)
    return total[None]


def solution(mesh):
    return jax.shard_map(
        local,
        mesh=mesh,
        in_specs=(P(("walkers", "band"), None, None),),
        out_specs=P(("walkers", "band"), None, None),
        check_vma=False,
    )
```

```python
import functools
import math

import jax
import jax.numpy as jnp
import ml_dtypes
import numpy as np
from jax import lax
from jax.experimental import pallas as pl
from jax.experimental.pallas import tpu as pltpu
from jax.sharding import PartitionSpec as P

NG = 64
HALF = 32
LANES = 128
SLOTS = 4
PITCH = 129
ROWS = 64 * PITCH + LANES
PARTS = 2
MIXING = 0.25


def dft_tables():
    index_row = np.arange(NG)
    angle = (index_row[:, None] * index_row[None, :] % NG).astype(np.float32)
    angle = angle * np.float32(2.0 * math.pi / NG)
    return [f(angle).astype(ml_dtypes.bfloat16).astype(np.float32) for f in (np.cos, np.sin)]


def paired(table_cos, table_sin, sign):
    return np.block([[table_cos, sign * table_sin], [-sign * table_sin, table_cos]])


def make_tables():
    cosine, sine = dft_tables()
    into = np.zeros((SLOTS, 2, NG, 2, 2, SLOTS, HALF), np.float32)
    back = np.zeros((2, 2, SLOTS, HALF, SLOTS, 2, NG), np.float32)
    for band in range(SLOTS):
        even = band - band % 2
        for parity in range(2):
            into[band, parity, :, parity, 0, band, 1:] = cosine[:, 1:HALF]
            into[band, parity, :, parity, 1, band, 1:] = -sine[:, 1:HALF]
            back[parity, 0, band, 1:, band, parity, :] = 2 * cosine[1:HALF]
            back[parity, 1, band, 1:, band, parity, :] = -2 * sine[1:HALF]
            for place, plane in ((even, 0), (even + 1, HALF)):
                into[band, parity, :, parity, band % 2, place, 0] = cosine[:, plane]
                back[parity, band % 2, place, 0, band, parity, :] = cosine[plane]
    wide = 2 * LANES
    into_low = into[:2, :, :, :, :, :2].reshape(wide, wide)
    into_high = into[2:, :, :, :, ::-1, 2:].reshape(wide, wide)
    back_low = back[:, :, :2, :, :2].reshape(wide, wide)
    back_high = back[:, ::-1, 2:, :, 2:].reshape(wide, wide)
    order = np.arange(NG).reshape(HALF, 2).T
    y_in = np.concatenate([np.concatenate([order[b] + NG * c for c in range(2)]) for b in range(2)])
    forward = paired(cosine, sine, 1.0)
    inverse = paired(cosine, sine, -1.0)
    wave = np.arange(NG)
    wave = np.where(wave < HALF, wave, wave - NG)
    slots = np.tile(np.arange(HALF), (SLOTS, 1))
    slots[1::2, 0] = HALF
    squared = wave[:, None, None] ** 2 + wave[None, :, None] ** 2 + slots.reshape(-1)[None, None, :] ** 2
    strength = np.float32(NG**1.5 / 4.0)
    kernel = np.where(squared > 0, strength / np.maximum(squared, 1).astype(np.float32), np.float32(0))
    as_bf = lambda table: table.astype(ml_dtypes.bfloat16)
    return (
        as_bf(into_low),
        as_bf(into_high),
        as_bf(forward[:, y_in]),
        as_bf(forward),
        kernel.reshape(NG * NG, LANES).astype(np.float32),
        as_bf(inverse),
        as_bf(inverse[y_in]),
        as_bf(back_low * np.float32(-MIXING / NG**3)),
        as_bf(back_high * np.float32(-MIXING / NG**3)),
    )


def dot(left, right):
    return jnp.dot(left, right, preferred_element_type=jnp.float32)


def forward_stages(own_ref, ahead_ref, behind_ref, into_low, into_high, y_fwd, x_fwd, kernel, x_inv, planes, spec, flat):
    block, x_unroll = NG, HALF
    rows = block * HALF
    low = lax.broadcasted_iota(jnp.int32, (rows, LANES), 1) < NG

    def wide(ref, base):
        return ref[pl.ds(base, rows), :].astype(jnp.float32)

    @pl.loop(0, 1)
    def _(at):
        base = pl.multiple_of(at * rows, rows)
        own, ahead, behind = (wide(ref, base) for ref in (own_ref, ahead_ref, behind_ref))
        density = [own * own, own * ahead, behind * own, behind * ahead]
        density = [d.astype(jnp.bfloat16) for d in density]
        first = dot(jnp.concatenate(density[:2], axis=1), into_low[...])
        other = dot(jnp.concatenate(density[2:], axis=1), into_high[...])
        for parity in range(2):
            lanes = slice(parity * LANES, (parity + 1) * LANES)
            one, two = (x[:, lanes].astype(jnp.bfloat16) for x in (first, other))
            real = jnp.where(low, one, two)
            imag = jnp.where(low, two, one)
            imag = jnp.concatenate([imag[:, NG:], imag[:, :NG]], axis=1)
            flat[:, 2 * parity * LANES : (2 * parity + 1) * LANES] = real
            flat[:, (2 * parity + 1) * LANES : (2 * parity + 2) * LANES] = imag
        for pair in range(block // 2):
            section = []
            for x in (2 * pair, 2 * pair + 1):
                section.append(
                    jnp.concatenate(
                        [flat[x * HALF : (x + 1) * HALF, t * LANES : (t + 1) * LANES] for t in range(4)], axis=0
                    )
                )
            second = dot(y_fwd[...], jnp.concatenate(section, axis=1))
            for n in range(2):
                place = (at * block + 2 * pair + n) * PITCH
                planes[pl.ds(place, LANES), :] = second[:, n * LANES : (n + 1) * LANES]

    @pl.loop(0, NG // (2 * x_unroll))
    def _(at):
        for pair in range(x_unroll):
            ky = (at * x_unroll + pair) * 2
            section = jnp.concatenate(
                [
                    jnp.concatenate(
                        [planes[pl.ds(ky + n + c * NG, NG, stride=PITCH), :] for c in range(2)], axis=0
                    ).astype(jnp.bfloat16)
                    for n in range(2)
                ],
                axis=1,
            )
            spectrum = dot(x_fwd[...], section)
            weight = jnp.concatenate(
                [kernel[pl.ds(pl.multiple_of((ky + n) * NG, NG), NG), :] for n in range(2)], axis=1
            )
            weight = jnp.concatenate([weight, weight], axis=0)
            spectrum = (spectrum * weight).astype(jnp.bfloat16)
            back_one = dot(x_inv[...], spectrum)
            for n in range(2):
                spec[pl.ds((ky + n) * PITCH, LANES), :] = back_one[:, n * LANES : (n + 1) * LANES]


def last_stages(part, parts, own_ref, ahead_ref, behind_ref, y_inv, back_low, back_high, spec, outputs, flat):
    out_ref, to_ahead, to_behind = outputs
    block = NG // parts
    rows = block * HALF
    low = lax.broadcasted_iota(jnp.int32, (rows, LANES), 1) < NG

    def wide(ref, base):
        return ref[pl.ds(base, rows), :].astype(jnp.float32)

    @pl.loop(part, part + 1)
    def _(at):
        for pair in range(block // 2):
            x = at * block + 2 * pair
            section = jnp.concatenate(
                [
                    jnp.concatenate(
                        [spec[pl.ds(x + n + c * NG, NG, stride=PITCH), :] for c in range(2)], axis=0
                    ).astype(jnp.bfloat16)
                    for n in range(2)
                ],
                axis=1,
            )
            back_two = dot(y_inv[...], section).astype(jnp.bfloat16)
            for n in range(2):
                row = (2 * pair + n) * HALF
                for parity in range(2):
                    lanes = slice(n * LANES, (n + 1) * LANES)
                    real = back_two[2 * parity * HALF : (2 * parity + 1) * HALF, lanes]
                    imag = back_two[(2 * parity + 1) * HALF : (2 * parity + 2) * HALF, lanes]
                    imag = jnp.concatenate([imag[:, NG:], imag[:, :NG]], axis=1)
                    for half, pick in enumerate((jnp.where(low[:HALF], real, imag), jnp.where(low[:HALF], imag, real))):
                        place = (2 * half + parity) * LANES
                        flat[row : row + HALF, place : place + LANES] = pick
        base = pl.multiple_of(at * rows, rows)
        alone, onward = jnp.split(dot(flat[:rows, : 2 * LANES], back_low[...]), 2, axis=1)
        rearward, across = jnp.split(dot(flat[:rows, 2 * LANES :], back_high[...]), 2, axis=1)
        own, ahead, behind = (wide(ref, base) for ref in (own_ref, ahead_ref, behind_ref))
        to_ahead[...] = (own * onward + behind * across).astype(jnp.bfloat16)
        to_behind[...] = (own * rearward + ahead * across).astype(jnp.bfloat16)
        out_ref[...] = own * alone + ahead * onward + behind * rearward


def first_kernel(*refs):
    orbitals, refs = refs[:3], refs[3:]
    into_low, into_high, y_fwd, x_fwd, kernel, x_inv, y_inv, back_low, back_high, *refs = refs
    *outputs, spec, planes, flat = refs
    forward_stages(*orbitals, into_low, into_high, y_fwd, x_fwd, kernel, x_inv, planes, spec, flat)
    last_stages(0, PARTS, *orbitals, y_inv, back_low, back_high, spec, outputs, flat)


def second_kernel(part, *refs):
    orbitals, refs = refs[:3], refs[3:]
    y_inv, back_low, back_high, spec, *refs = refs
    *outputs, flat = refs
    last_stages(part, PARTS, *orbitals, y_inv, back_low, back_high, spec, outputs, flat)


def finish_kernel(*refs):
    groups, out_ref, held, sem = refs[:-3], refs[-3], refs[-2], refs[-1]
    rows = groups[0].shape[0]
    copies = []
    for n in range(len(groups) // 3):
        total, one, two = groups[3 * n : 3 * n + 3]
        for half in range(2):
            here = pl.ds(half * (rows // 2), rows // 2)
            there = pl.ds(n * rows + half * (rows // 2), rows // 2)
            held[there, :] = total[here, :] + one[here, :].astype(jnp.float32) + two[here, :].astype(jnp.float32)
            copies.append(pltpu.make_async_copy(held.at[there], out_ref.at[there], sem.at[2 * n + half]))
            copies[-1].start()
    for copy in copies:
        copy.wait()


def hold_kernel(*refs):
    count = len(refs) // 2
    sources, held, sem = refs[:count], refs[count : 2 * count], refs[2 * count]
    copies = [pltpu.make_async_copy(s, h, sem.at[n]) for n, (s, h) in enumerate(zip(sources, held))]
    for copy in copies:
        copy.start()
    for copy in copies:
        copy.wait()


def held_in_vmem(arrays):
    return pl.pallas_call(
        hold_kernel,
        out_shape=[pltpu.VMEM(x.shape, x.dtype) for x in arrays],
        in_specs=[pl.BlockSpec(memory_space=pl.ANY)] * len(arrays),
        out_specs=[pl.BlockSpec(memory_space=pltpu.VMEM)] * len(arrays),
        scratch_shapes=[pltpu.SemaphoreType.DMA((len(arrays),))],
        compiler_params=pltpu.CompilerParams(vmem_limit_bytes=1024 * 1024),
        cost_estimate=pl.CostEstimate(flops=0, bytes_accessed=8 << 20, transcendentals=0),
    )(*arrays)


def vmem_call(kernel, outputs, scratch, operands, flops):
    return pl.pallas_call(
        kernel,
        out_shape=outputs,
        in_specs=[pl.BlockSpec(memory_space=pltpu.VMEM)] * len(operands),
        out_specs=[pl.BlockSpec(memory_space=pltpu.VMEM)] * len(outputs),
        scratch_shapes=scratch,
        compiler_params=pltpu.CompilerParams(vmem_limit_bytes=24 * 1024 * 1024),
        cost_estimate=pl.CostEstimate(flops=flops, bytes_accessed=8 << 20, transcendentals=0),
    )(*operands)


def finished(groups, rows):
    operands = [x for group in groups for x in group]
    return pl.pallas_call(
        finish_kernel,
        out_shape=jax.ShapeDtypeStruct((rows, LANES), jnp.float32),
        in_specs=[pl.BlockSpec(memory_space=pltpu.VMEM)] * len(operands),
        out_specs=pl.BlockSpec(memory_space=pl.ANY),
        scratch_shapes=[pltpu.VMEM((rows, LANES), jnp.float32), pltpu.SemaphoreType.DMA((2 * len(groups),))],
        compiler_params=pltpu.CompilerParams(vmem_limit_bytes=16 * 1024 * 1024),
        cost_estimate=pl.CostEstimate(flops=2**20, bytes_accessed=3 << 20, transcendentals=0),
    )(*operands)


def shifted(x, by):
    count = lax.axis_size("band")
    return lax.ppermute(x, "band", [(i, (i + by) % count) for i in range(count)])


def local(orbitals):
    rows = orbitals.shape[1]
    behind = shifted(orbitals[0], 1)
    ahead = shifted(orbitals[0], -2)
    own, *tables = held_in_vmem([orbitals[0], *(jnp.asarray(t) for t in make_tables())])
    part = [pltpu.VMEM((rows // PARTS, LANES), t) for t in (jnp.float32, jnp.bfloat16, jnp.bfloat16)]
    planes = pltpu.VMEM((ROWS, LANES), jnp.float32)
    scratch = [planes, pltpu.VMEM((rows, SLOTS * LANES), jnp.bfloat16)]
    *terms, spec = vmem_call(first_kernel, part + [planes], scratch, [own, ahead, behind, *tables], 2**32)
    groups = []
    for n in range(PARTS):
        if n > 0:
            operands = [own, ahead, behind, *tables[-3:], spec]
            terms = vmem_call(functools.partial(second_kernel, n), part, scratch[1:], operands, 2**30)
        total, to_ahead, to_behind = terms
        groups.append([total, shifted(to_ahead, 2), shifted(to_behind, -1)])
    return finished(groups, rows)[None]


def solution(mesh):
    return jax.shard_map(
        local,
        mesh=mesh,
        in_specs=(P(("walkers", "band"), None, None),),
        out_specs=P(("walkers", "band"), None, None),
        check_vma=False,
    )
```

```python
import functools
import math

import jax
import jax.numpy as jnp
import ml_dtypes
import numpy as np
from jax import lax
from jax.experimental import pallas as pl
from jax.experimental.pallas import tpu as pltpu
from jax.sharding import PartitionSpec as P

NG = 64
HALF = 32
LANES = 128
SLOTS = 4
PITCH = 129
ROWS = 64 * PITCH + LANES
PARTS = 2
CHUNKS = 2
MIXING = 0.25


def dft_tables():
    index_row = np.arange(NG)
    angle = (index_row[:, None] * index_row[None, :] % NG).astype(np.float32)
    angle = angle * np.float32(2.0 * math.pi / NG)
    return [f(angle).astype(ml_dtypes.bfloat16).astype(np.float32) for f in (np.cos, np.sin)]


def paired(table_cos, table_sin, sign):
    return np.block([[table_cos, sign * table_sin], [-sign * table_sin, table_cos]])


def make_tables():
    cosine, sine = dft_tables()
    into = np.zeros((SLOTS, 2, NG, 2, 2, SLOTS, HALF), np.float32)
    back = np.zeros((2, 2, SLOTS, HALF, SLOTS, 2, NG), np.float32)
    for band in range(SLOTS):
        even = band - band % 2
        for parity in range(2):
            into[band, parity, :, parity, 0, band, 1:] = cosine[:, 1:HALF]
            into[band, parity, :, parity, 1, band, 1:] = -sine[:, 1:HALF]
            back[parity, 0, band, 1:, band, parity, :] = 2 * cosine[1:HALF]
            back[parity, 1, band, 1:, band, parity, :] = -2 * sine[1:HALF]
            for place, plane in ((even, 0), (even + 1, HALF)):
                into[band, parity, :, parity, band % 2, place, 0] = cosine[:, plane]
                back[parity, band % 2, place, 0, band, parity, :] = cosine[plane]
    wide = 2 * LANES
    into_low = into[:2, :, :, :, :, :2].reshape(wide, wide)
    into_high = into[2:, :, :, :, ::-1, 2:].reshape(wide, wide)
    back_low = back[:, :, :2, :, :2].reshape(wide, wide)
    back_high = back[:, ::-1, 2:, :, 2:].reshape(wide, wide)
    order = np.arange(NG).reshape(HALF, 2).T
    y_in = np.concatenate([np.concatenate([order[b] + NG * c for c in range(2)]) for b in range(2)])
    forward = paired(cosine, sine, 1.0)
    inverse = paired(cosine, sine, -1.0)
    wave = np.arange(NG)
    wave = np.where(wave < HALF, wave, wave - NG)
    slots = np.tile(np.arange(HALF), (SLOTS, 1))
    slots[1::2, 0] = HALF
    squared = wave[:, None, None] ** 2 + wave[None, :, None] ** 2 + slots.reshape(-1)[None, None, :] ** 2
    strength = np.float32(NG**1.5 / 4.0)
    kernel = np.where(squared > 0, strength / np.maximum(squared, 1).astype(np.float32), np.float32(0))
    as_bf = lambda table: table.astype(ml_dtypes.bfloat16)
    return (
        as_bf(into_low),
        as_bf(into_high),
        as_bf(forward[:, y_in]),
        as_bf(forward),
        kernel.reshape(NG * NG, LANES).astype(np.float32),
        as_bf(inverse),
        as_bf(inverse[y_in]),
        as_bf(back_low * np.float32(-MIXING / NG**3)),
        as_bf(back_high * np.float32(-MIXING / NG**3)),
    )


def dot(left, right):
    return jnp.dot(left, right, preferred_element_type=jnp.float32)


def forward_stages(own_ref, ahead_ref, behind_ref, into_low, into_high, y_fwd, x_fwd, kernel, x_inv, planes, spec, flat):
    block, x_unroll = NG, HALF
    rows = block * HALF
    low = lax.broadcasted_iota(jnp.int32, (rows, LANES), 1) < NG

    def wide(ref, base):
        return ref[pl.ds(base, rows), :].astype(jnp.float32)

    @pl.loop(0, 1)
    def _(at):
        base = pl.multiple_of(at * rows, rows)
        own, ahead, behind = (wide(ref, base) for ref in (own_ref, ahead_ref, behind_ref))
        density = [own * own, own * ahead, behind * own, behind * ahead]
        density = [d.astype(jnp.bfloat16) for d in density]
        first = dot(jnp.concatenate(density[:2], axis=1), into_low[...])
        other = dot(jnp.concatenate(density[2:], axis=1), into_high[...])
        for parity in range(2):
            lanes = slice(parity * LANES, (parity + 1) * LANES)
            one, two = (x[:, lanes].astype(jnp.bfloat16) for x in (first, other))
            real = jnp.where(low, one, two)
            imag = jnp.where(low, two, one)
            imag = jnp.concatenate([imag[:, NG:], imag[:, :NG]], axis=1)
            flat[:, 2 * parity * LANES : (2 * parity + 1) * LANES] = real
            flat[:, (2 * parity + 1) * LANES : (2 * parity + 2) * LANES] = imag
        for pair in range(block // 2):
            section = []
            for x in (2 * pair, 2 * pair + 1):
                section.append(
                    jnp.concatenate(
                        [flat[x * HALF : (x + 1) * HALF, t * LANES : (t + 1) * LANES] for t in range(4)], axis=0
                    )
                )
            second = dot(y_fwd[...], jnp.concatenate(section, axis=1))
            for n in range(2):
                place = (at * block + 2 * pair + n) * PITCH
                planes[pl.ds(place, LANES), :] = second[:, n * LANES : (n + 1) * LANES]

    @pl.loop(0, NG // (2 * x_unroll))
    def _(at):
        for pair in range(x_unroll):
            ky = (at * x_unroll + pair) * 2
            section = jnp.concatenate(
                [
                    jnp.concatenate(
                        [planes[pl.ds(ky + n + c * NG, NG, stride=PITCH), :] for c in range(2)], axis=0
                    ).astype(jnp.bfloat16)
                    for n in range(2)
                ],
                axis=1,
            )
            spectrum = dot(x_fwd[...], section)
            weight = jnp.concatenate(
                [kernel[pl.ds(pl.multiple_of((ky + n) * NG, NG), NG), :] for n in range(2)], axis=1
            )
            weight = jnp.concatenate([weight, weight], axis=0)
            spectrum = (spectrum * weight).astype(jnp.bfloat16)
            back_one = dot(x_inv[...], spectrum)
            for n in range(2):
                spec[pl.ds((ky + n) * PITCH, LANES), :] = back_one[:, n * LANES : (n + 1) * LANES]


def last_stages(part, parts, own_ref, ahead_ref, behind_ref, y_inv, back_low, back_high, spec, outputs, flat):
    out_ref, to_ahead, to_behind = outputs
    block = NG // parts
    rows = block * HALF
    low = lax.broadcasted_iota(jnp.int32, (rows, LANES), 1) < NG

    def wide(ref, base):
        return ref[pl.ds(base, rows), :].astype(jnp.float32)

    @pl.loop(part, part + 1)
    def _(at):
        for pair in range(block // 2):
            x = at * block + 2 * pair
            section = jnp.concatenate(
                [
                    jnp.concatenate(
                        [spec[pl.ds(x + n + c * NG, NG, stride=PITCH), :] for c in range(2)], axis=0
                    ).astype(jnp.bfloat16)
                    for n in range(2)
                ],
                axis=1,
            )
            back_two = dot(y_inv[...], section).astype(jnp.bfloat16)
            for n in range(2):
                row = (2 * pair + n) * HALF
                for parity in range(2):
                    lanes = slice(n * LANES, (n + 1) * LANES)
                    real = back_two[2 * parity * HALF : (2 * parity + 1) * HALF, lanes]
                    imag = back_two[(2 * parity + 1) * HALF : (2 * parity + 2) * HALF, lanes]
                    imag = jnp.concatenate([imag[:, NG:], imag[:, :NG]], axis=1)
                    for half, pick in enumerate((jnp.where(low[:HALF], real, imag), jnp.where(low[:HALF], imag, real))):
                        place = (2 * half + parity) * LANES
                        flat[row : row + HALF, place : place + LANES] = pick
        base = pl.multiple_of(at * rows, rows)
        alone, onward = jnp.split(dot(flat[:rows, : 2 * LANES], back_low[...]), 2, axis=1)
        rearward, across = jnp.split(dot(flat[:rows, 2 * LANES :], back_high[...]), 2, axis=1)
        own, ahead, behind = (wide(ref, base) for ref in (own_ref, ahead_ref, behind_ref))
        to_ahead[...] = (own * onward + behind * across).astype(jnp.bfloat16)
        to_behind[...] = (own * rearward + ahead * across).astype(jnp.bfloat16)
        out_ref[...] = own * alone + ahead * onward + behind * rearward


def first_kernel(*refs):
    orbitals, refs = refs[:3], refs[3:]
    into_low, into_high, y_fwd, x_fwd, kernel, x_inv, y_inv, back_low, back_high, *refs = refs
    *outputs, spec, planes, flat = refs
    forward_stages(*orbitals, into_low, into_high, y_fwd, x_fwd, kernel, x_inv, planes, spec, flat)
    last_stages(0, PARTS, *orbitals, y_inv, back_low, back_high, spec, outputs, flat)


def second_kernel(part, *refs):
    orbitals, refs = refs[:3], refs[3:]
    y_inv, back_low, back_high, spec, *refs = refs
    *outputs, flat = refs
    last_stages(part, PARTS, *orbitals, y_inv, back_low, back_high, spec, outputs, flat)


def finish_kernel(part, total, one, two, *refs):
    out_ref, held, sem = refs[-3:]
    rows = total.shape[0] // CHUNKS
    copies = []
    for n in range(CHUNKS):
        here = pl.ds(n * rows, rows)
        there = pl.ds((part * CHUNKS + n) * rows, rows)
        held[here, :] = total[here, :] + one[here, :].astype(jnp.float32) + two[here, :].astype(jnp.float32)
        copies.append(pltpu.make_async_copy(held.at[here], out_ref.at[there], sem.at[n]))
        copies[-1].start()
    for copy in copies:
        copy.wait()


def hold_kernel(*refs):
    count = len(refs) // 2
    sources, held, sem = refs[:count], refs[count : 2 * count], refs[2 * count]
    copies = [pltpu.make_async_copy(s, h, sem.at[n]) for n, (s, h) in enumerate(zip(sources, held))]
    for copy in copies:
        copy.start()
    for copy in copies:
        copy.wait()


def held_in_vmem(arrays):
    return pl.pallas_call(
        hold_kernel,
        out_shape=[pltpu.VMEM(x.shape, x.dtype) for x in arrays],
        in_specs=[pl.BlockSpec(memory_space=pl.ANY)] * len(arrays),
        out_specs=[pl.BlockSpec(memory_space=pltpu.VMEM)] * len(arrays),
        scratch_shapes=[pltpu.SemaphoreType.DMA((len(arrays),))],
        compiler_params=pltpu.CompilerParams(vmem_limit_bytes=1024 * 1024),
        cost_estimate=pl.CostEstimate(flops=0, bytes_accessed=8 << 20, transcendentals=0),
    )(*arrays)


def vmem_call(kernel, outputs, scratch, operands, flops):
    return pl.pallas_call(
        kernel,
        out_shape=outputs,
        in_specs=[pl.BlockSpec(memory_space=pltpu.VMEM)] * len(operands),
        out_specs=[pl.BlockSpec(memory_space=pltpu.VMEM)] * len(outputs),
        scratch_shapes=scratch,
        compiler_params=pltpu.CompilerParams(vmem_limit_bytes=24 * 1024 * 1024),
        cost_estimate=pl.CostEstimate(flops=flops, bytes_accessed=8 << 20, transcendentals=0),
    )(*operands)


def finished(part, terms, earlier):
    rows = terms[0].shape[0]
    return pl.pallas_call(
        functools.partial(finish_kernel, part),
        out_shape=jax.ShapeDtypeStruct((PARTS * rows, LANES), jnp.float32),
        in_specs=[pl.BlockSpec(memory_space=pltpu.VMEM)] * 3 + [pl.BlockSpec(memory_space=pl.ANY)] * len(earlier),
        out_specs=pl.BlockSpec(memory_space=pl.ANY),
        scratch_shapes=[pltpu.VMEM((rows, LANES), jnp.float32), pltpu.SemaphoreType.DMA((CHUNKS,))],
        input_output_aliases={3: 0} if earlier else {},
        compiler_params=pltpu.CompilerParams(vmem_limit_bytes=16 * 1024 * 1024),
        cost_estimate=pl.CostEstimate(flops=2**20, bytes_accessed=2 << 20, transcendentals=0),
    )(*terms, *earlier)


def shifted(x, by):
    count = lax.axis_size("band")
    return lax.ppermute(x, "band", [(i, (i + by) % count) for i in range(count)])


def local(orbitals):
    rows = orbitals.shape[1]
    behind = shifted(orbitals[0], 1)
    ahead = shifted(orbitals[0], -2)
    own, *tables = held_in_vmem([orbitals[0], *(jnp.asarray(t) for t in make_tables())])
    part = [pltpu.VMEM((rows // PARTS, LANES), t) for t in (jnp.float32, jnp.bfloat16, jnp.bfloat16)]
    planes = pltpu.VMEM((ROWS, LANES), jnp.float32)
    scratch = [planes, pltpu.VMEM((rows, SLOTS * LANES), jnp.bfloat16)]
    *terms, spec = vmem_call(first_kernel, part + [planes], scratch, [own, ahead, behind, *tables], 2**32)
    groups = []
    for n in range(PARTS):
        if n > 0:
            operands = [own, ahead, behind, *tables[-3:], spec]
            terms = vmem_call(functools.partial(second_kernel, n), part, scratch[1:], operands, 2**30)
        total, to_ahead, to_behind = terms
        groups.append([total, shifted(to_ahead, 2), shifted(to_behind, -1)])
    out = []
    for n, group in enumerate(groups):
        out = [finished(n, group, out)]
    return out[0][None]


def solution(mesh):
    return jax.shard_map(
        local,
        mesh=mesh,
        in_specs=(P(("walkers", "band"), None, None),),
        out_specs=P(("walkers", "band"), None, None),
        check_vma=False,
    )
```

```python
import functools
import math

import jax
import jax.numpy as jnp
import ml_dtypes
import numpy as np
from jax import lax
from jax.experimental import pallas as pl
from jax.experimental.pallas import tpu as pltpu
from jax.sharding import PartitionSpec as P

NG = 64
HALF = 32
LANES = 128
SLOTS = 4
PITCH = 129
ROWS = 64 * PITCH + LANES
PARTS = 2
CHUNKS = 2
MIXING = 0.25


def dft_tables():
    index_row = np.arange(NG)
    angle = (index_row[:, None] * index_row[None, :] % NG).astype(np.float32)
    angle = angle * np.float32(2.0 * math.pi / NG)
    return [f(angle).astype(ml_dtypes.bfloat16).astype(np.float32) for f in (np.cos, np.sin)]


def paired(table_cos, table_sin, sign):
    return np.block([[table_cos, sign * table_sin], [-sign * table_sin, table_cos]])


def make_tables():
    cosine, sine = dft_tables()
    into = np.zeros((SLOTS, 2, NG, 2, 2, SLOTS, HALF), np.float32)
    back = np.zeros((2, 2, SLOTS, HALF, SLOTS, 2, NG), np.float32)
    for band in range(SLOTS):
        even = band - band % 2
        for parity in range(2):
            into[band, parity, :, parity, 0, band, 1:] = cosine[:, 1:HALF]
            into[band, parity, :, parity, 1, band, 1:] = -sine[:, 1:HALF]
            back[parity, 0, band, 1:, band, parity, :] = 2 * cosine[1:HALF]
            back[parity, 1, band, 1:, band, parity, :] = -2 * sine[1:HALF]
            for place, plane in ((even, 0), (even + 1, HALF)):
                into[band, parity, :, parity, band % 2, place, 0] = cosine[:, plane]
                back[parity, band % 2, place, 0, band, parity, :] = cosine[plane]
    wide = 2 * LANES
    into_low = into[:2, :, :, :, :, :2].reshape(wide, wide)
    into_high = into[2:, :, :, :, ::-1, 2:].reshape(wide, wide)
    back_low = back[:, :, :2, :, :2].reshape(wide, wide)
    back_high = back[:, ::-1, 2:, :, 2:].reshape(wide, wide)
    order = np.arange(NG).reshape(HALF, 2).T
    y_in = np.concatenate([np.concatenate([order[b] + NG * c for c in range(2)]) for b in range(2)])
    forward = paired(cosine, sine, 1.0)
    inverse = paired(cosine, sine, -1.0)
    wave = np.arange(NG)
    wave = np.where(wave < HALF, wave, wave - NG)
    slots = np.tile(np.arange(HALF), (SLOTS, 1))
    slots[1::2, 0] = HALF
    squared = wave[:, None, None] ** 2 + wave[None, :, None] ** 2 + slots.reshape(-1)[None, None, :] ** 2
    strength = np.float32(NG**1.5 / 4.0)
    kernel = np.where(squared > 0, strength / np.maximum(squared, 1).astype(np.float32), np.float32(0))
    as_bf = lambda table: table.astype(ml_dtypes.bfloat16)
    return (
        as_bf(into_low),
        as_bf(into_high),
        as_bf(forward[:, y_in]),
        as_bf(forward),
        kernel.reshape(NG * NG, LANES).astype(np.float32),
        as_bf(inverse),
        as_bf(inverse[y_in]),
        as_bf(back_low * np.float32(-MIXING / NG**3)),
        as_bf(back_high * np.float32(-MIXING / NG**3)),
    )


def dot(left, right):
    return jnp.dot(left, right, preferred_element_type=jnp.float32)


def forward_stages(own_ref, ahead_ref, behind_ref, into_low, into_high, y_fwd, x_fwd, kernel, x_inv, planes, spec, flat):
    block, x_unroll = NG, HALF
    rows = block * HALF
    low = lax.broadcasted_iota(jnp.int32, (rows, LANES), 1) < NG

    def wide(ref, base):
        return ref[pl.ds(base, rows), :].astype(jnp.float32)

    @pl.loop(0, 1)
    def _(at):
        base = pl.multiple_of(at * rows, rows)
        own, ahead, behind = (wide(ref, base) for ref in (own_ref, ahead_ref, behind_ref))
        density = [own * own, own * ahead, behind * own, behind * ahead]
        density = [d.astype(jnp.bfloat16) for d in density]
        first = dot(jnp.concatenate(density[:2], axis=1), into_low[...])
        other = dot(jnp.concatenate(density[2:], axis=1), into_high[...])
        for parity in range(2):
            lanes = slice(parity * LANES, (parity + 1) * LANES)
            one, two = (x[:, lanes].astype(jnp.bfloat16) for x in (first, other))
            real = jnp.where(low, one, two)
            imag = jnp.where(low, two, one)
            imag = jnp.concatenate([imag[:, NG:], imag[:, :NG]], axis=1)
            flat[:, 2 * parity * LANES : (2 * parity + 1) * LANES] = real
            flat[:, (2 * parity + 1) * LANES : (2 * parity + 2) * LANES] = imag
        for pair in range(block // 2):
            section = []
            for x in (2 * pair, 2 * pair + 1):
                section.append(
                    jnp.concatenate(
                        [flat[x * HALF : (x + 1) * HALF, t * LANES : (t + 1) * LANES] for t in range(4)], axis=0
                    )
                )
            second = dot(y_fwd[...], jnp.concatenate(section, axis=1))
            for n in range(2):
                place = (at * block + 2 * pair + n) * PITCH
                planes[pl.ds(place, LANES), :] = second[:, n * LANES : (n + 1) * LANES]

    @pl.loop(0, NG // (2 * x_unroll))
    def _(at):
        for pair in range(x_unroll):
            ky = (at * x_unroll + pair) * 2
            section = jnp.concatenate(
                [
                    jnp.concatenate(
                        [planes[pl.ds(ky + n + c * NG, NG, stride=PITCH), :] for c in range(2)], axis=0
                    ).astype(jnp.bfloat16)
                    for n in range(2)
                ],
                axis=1,
            )
            spectrum = dot(x_fwd[...], section)
            weight = jnp.concatenate(
                [kernel[pl.ds(pl.multiple_of((ky + n) * NG, NG), NG), :] for n in range(2)], axis=1
            )
            weight = jnp.concatenate([weight, weight], axis=0)
            spectrum = (spectrum * weight).astype(jnp.bfloat16)
            back_one = dot(x_inv[...], spectrum)
            for n in range(2):
                spec[pl.ds((ky + n) * PITCH, LANES), :] = back_one[:, n * LANES : (n + 1) * LANES]


def last_stages(part, parts, own_ref, ahead_ref, behind_ref, y_inv, back_low, back_high, spec, outputs, flat):
    out_ref, to_ahead, to_behind = outputs
    block = NG // parts
    rows = block * HALF
    low = lax.broadcasted_iota(jnp.int32, (rows, LANES), 1) < NG

    def wide(ref, base):
        return ref[pl.ds(base, rows), :].astype(jnp.float32)

    @pl.loop(part, part + 1)
    def _(at):
        for pair in range(block // 2):
            x = at * block + 2 * pair
            section = jnp.concatenate(
                [
                    jnp.concatenate(
                        [spec[pl.ds(x + n + c * NG, NG, stride=PITCH), :] for c in range(2)], axis=0
                    ).astype(jnp.bfloat16)
                    for n in range(2)
                ],
                axis=1,
            )
            back_two = dot(y_inv[...], section).astype(jnp.bfloat16)
            for n in range(2):
                row = (2 * pair + n) * HALF
                for parity in range(2):
                    lanes = slice(n * LANES, (n + 1) * LANES)
                    real = back_two[2 * parity * HALF : (2 * parity + 1) * HALF, lanes]
                    imag = back_two[(2 * parity + 1) * HALF : (2 * parity + 2) * HALF, lanes]
                    imag = jnp.concatenate([imag[:, NG:], imag[:, :NG]], axis=1)
                    for half, pick in enumerate((jnp.where(low[:HALF], real, imag), jnp.where(low[:HALF], imag, real))):
                        place = (2 * half + parity) * LANES
                        flat[row : row + HALF, place : place + LANES] = pick
        base = pl.multiple_of(at * rows, rows)
        alone, onward = jnp.split(dot(flat[:rows, : 2 * LANES], back_low[...]), 2, axis=1)
        rearward, across = jnp.split(dot(flat[:rows, 2 * LANES :], back_high[...]), 2, axis=1)
        own, ahead, behind = (wide(ref, base) for ref in (own_ref, ahead_ref, behind_ref))
        to_ahead[...] = (own * onward + behind * across).astype(jnp.bfloat16)
        to_behind[...] = (own * rearward + ahead * across).astype(jnp.bfloat16)
        out_ref[...] = own * alone + ahead * onward + behind * rearward


def first_kernel(*refs):
    orbitals, refs = refs[:3], refs[3:]
    wide_tables, narrow_tables, kernel, *refs = refs
    into_low, into_high, back_low, back_high = (wide_tables.at[n] for n in range(4))
    y_fwd, x_fwd, x_inv, y_inv = (narrow_tables.at[n] for n in range(4))
    *outputs, spec, planes, flat = refs
    forward_stages(*orbitals, into_low, into_high, y_fwd, x_fwd, kernel, x_inv, planes, spec, flat)
    last_stages(0, PARTS, *orbitals, y_inv, back_low, back_high, spec, outputs, flat)


def second_kernel(part, *refs):
    orbitals, refs = refs[:3], refs[3:]
    wide_tables, narrow_tables, spec, *refs = refs
    y_inv, back_low, back_high = narrow_tables.at[3], wide_tables.at[2], wide_tables.at[3]
    *outputs, flat = refs
    last_stages(part, PARTS, *orbitals, y_inv, back_low, back_high, spec, outputs, flat)


def finish_kernel(part, total, one, two, *refs):
    out_ref, held, sem = refs[-3:]
    rows = total.shape[0] // CHUNKS
    copies = []
    for n in range(CHUNKS):
        here = pl.ds(n * rows, rows)
        there = pl.ds((part * CHUNKS + n) * rows, rows)
        held[here, :] = total[here, :] + one[here, :].astype(jnp.float32) + two[here, :].astype(jnp.float32)
        copies.append(pltpu.make_async_copy(held.at[here], out_ref.at[there], sem.at[n]))
        copies[-1].start()
    for copy in copies:
        copy.wait()


def hold_kernel(*refs):
    count = len(refs) // 2
    sources, held, sem = refs[:count], refs[count : 2 * count], refs[2 * count]
    copies = [pltpu.make_async_copy(s, h, sem.at[n]) for n, (s, h) in enumerate(zip(sources, held))]
    for copy in copies:
        copy.start()
    for copy in copies:
        copy.wait()


def held_in_vmem(arrays):
    return pl.pallas_call(
        hold_kernel,
        out_shape=[pltpu.VMEM(x.shape, x.dtype) for x in arrays],
        in_specs=[pl.BlockSpec(memory_space=pl.ANY)] * len(arrays),
        out_specs=[pl.BlockSpec(memory_space=pltpu.VMEM)] * len(arrays),
        scratch_shapes=[pltpu.SemaphoreType.DMA((len(arrays),))],
        compiler_params=pltpu.CompilerParams(vmem_limit_bytes=1024 * 1024),
        cost_estimate=pl.CostEstimate(flops=0, bytes_accessed=8 << 20, transcendentals=0),
    )(*arrays)


def vmem_call(kernel, outputs, scratch, operands, flops):
    return pl.pallas_call(
        kernel,
        out_shape=outputs,
        in_specs=[pl.BlockSpec(memory_space=pltpu.VMEM)] * len(operands),
        out_specs=[pl.BlockSpec(memory_space=pltpu.VMEM)] * len(outputs),
        scratch_shapes=scratch,
        compiler_params=pltpu.CompilerParams(vmem_limit_bytes=24 * 1024 * 1024),
        cost_estimate=pl.CostEstimate(flops=flops, bytes_accessed=8 << 20, transcendentals=0),
    )(*operands)


def finished(part, terms, earlier):
    rows = terms[0].shape[0]
    return pl.pallas_call(
        functools.partial(finish_kernel, part),
        out_shape=jax.ShapeDtypeStruct((PARTS * rows, LANES), jnp.float32),
        in_specs=[pl.BlockSpec(memory_space=pltpu.VMEM)] * 3 + [pl.BlockSpec(memory_space=pl.ANY)] * len(earlier),
        out_specs=pl.BlockSpec(memory_space=pl.ANY),
        scratch_shapes=[pltpu.VMEM((rows, LANES), jnp.float32), pltpu.SemaphoreType.DMA((CHUNKS,))],
        input_output_aliases={3: 0} if earlier else {},
        compiler_params=pltpu.CompilerParams(vmem_limit_bytes=16 * 1024 * 1024),
        cost_estimate=pl.CostEstimate(flops=2**20, bytes_accessed=2 << 20, transcendentals=0),
    )(*terms, *earlier)


def shifted(x, by):
    count = lax.axis_size("band")
    return lax.ppermute(x, "band", [(i, (i + by) % count) for i in range(count)])


def local(orbitals):
    rows = orbitals.shape[1]
    behind = shifted(orbitals[0], 1)
    ahead = shifted(orbitals[0], -2)
    t = make_tables()
    packed = np.stack([t[0], t[1], t[7], t[8]]), np.stack([t[2], t[3], t[5], t[6]]), t[4]
    own, *tables = held_in_vmem([orbitals[0], *(jnp.asarray(x) for x in packed)])
    part = [pltpu.VMEM((rows // PARTS, LANES), t) for t in (jnp.float32, jnp.bfloat16, jnp.bfloat16)]
    planes = pltpu.VMEM((ROWS, LANES), jnp.float32)
    scratch = [planes, pltpu.VMEM((rows, SLOTS * LANES), jnp.bfloat16)]
    *terms, spec = vmem_call(first_kernel, part + [planes], scratch, [own, ahead, behind, *tables], 2**32)
    groups = []
    for n in range(PARTS):
        if n > 0:
            operands = [own, ahead, behind, *tables[:2], spec]
            terms = vmem_call(functools.partial(second_kernel, n), part, scratch[1:], operands, 2**30)
        total, to_ahead, to_behind = terms
        groups.append([total, shifted(to_ahead, 2), shifted(to_behind, -1)])
    out = []
    for n, group in enumerate(groups):
        out = [finished(n, group, out)]
    return out[0][None]


def solution(mesh):
    return jax.shard_map(
        local,
        mesh=mesh,
        in_specs=(P(("walkers", "band"), None, None),),
        out_specs=P(("walkers", "band"), None, None),
        check_vma=False,
    )
```
